256 devices in a mesh: dp: 16 (over x, y), ctx: 16 (over z, core).
Axes of the slice: x: 4, y: 4, z: 8, core: 2. Of those that a mesh axis runs over, the one named last changes fastest.
Arguments:
- q_nope: bfloat16 [64, 128, 128], P('dp', 'ctx'), may hold values from -6 to 6
- q_rope: bfloat16 [64, 128, 64], P('dp', 'ctx'), may hold values from -8 to 8
- w_uk: bfloat16 [128, 128, 512], P('ctx'), may hold values from -0.5 to 0.5
- w_uv: bfloat16 [128, 512, 128], P('ctx'), may hold values from -6 to 6
- w_out: bfloat16 [16384, 7168], P('ctx', 'dp'), may hold values from -0.046875 to 0.046875
- latent_cache: bfloat16 [64, 32768, 576], P('dp', 'ctx'), may hold values from -8 to 8
- lengths: int32 [64], P('dp'), may hold values from 1 to 32768, as said below
Outputs:
- layer_out: bfloat16 [64, 7168], P('ctx', 'dp')
The draws below stay inside these ranges and needn't reach their ends.
Inputs may be any that keep to these rules, and one draw needn't show every extreme that they name: `lengths`: cached positions of each sequence; some sequence fills all 32768.
All inputs are finite; a program needn't handle non-finite values.
Results may differ from the reference program's by a relative error of at most 0.024.
Values may be sent and summed in bfloat16 or wider, within the bound.
A program may use at most 128 MiB of HBM per device.

```python
import math
import jax
import jax.numpy as jnp
from jax import lax

H = 128
LAT = 512
R = 64
DN = 128
DV = 128
D = 7168
B = 64
CTX = 32768


def draw_q_rope(key, part):
    key = jax.random.fold_in(key, 3)
    values = jnp.clip(jax.random.normal(key, (B, H, R), jnp.float32), -8.0, 8.0)
    return values.astype(jnp.bfloat16)


def draw_latent_cache(key, part):
    key = jax.random.fold_in(key, 11)
    values = jnp.clip(jax.random.normal(key, (B, CTX, LAT + R), jnp.float32), -8.0, 8.0)
    return values.astype(jnp.bfloat16)


def draw_lengths(key, part):
    key = jax.random.fold_in(key, 5)
    key_len, key_full = jax.random.split(key)
    counts = jax.random.randint(key_len, (B,), 1, CTX + 1)
    filled = jax.random.randint(key_full, (), 0, B)
    return jnp.where(jnp.arange(B, dtype=jnp.int32) == filled, CTX, counts).astype(jnp.int32)


def shard_levels(key, extent, pieces, low, top_value):
    def one(axis_at, blocks):
        draws = jax.random.uniform(jax.random.fold_in(jax.random.fold_in(key, 6), axis_at), (blocks,), jnp.float32, low / len(pieces), top_value / len(pieces))
        return jnp.repeat(jnp.exp(draws), extent[axis_at] // blocks).reshape((-1,) + (1,) * (len(extent) - axis_at - 1))

    gain = one(*pieces[0])
    for cut in pieces[1:]:
        gain = gain * one(*cut)
    return gain


def noise(own_key, shape, spread, bound, shards=(), kind=jnp.bfloat16):
    gain = shard_levels(own_key, shape, shards, -0.22, 0.18) if shards else 1.0
    drawn = jax.random.normal(own_key, shape, jnp.float32) * spread * gain
    return jnp.minimum(jnp.maximum(drawn, -bound), bound).astype(kind)


def setup_inputs(seed: int = 0) -> dict:
    key_of = jax.random.split(jax.random.key(seed), 8)
    q_nope = noise(key_of[0], (B, H, DN), 1.0, 6.0, ((0, 16), (1, 16)))
    q_rope = draw_q_rope(jax.random.fold_in(key_of[7], 71), 0)
    w_uk = noise(key_of[2], (H, DN, LAT), DN ** -0.5, 0.5, ((0, 16),))
    w_uv = noise(key_of[3], (H, LAT, DV), 1.0, 6.0, ((0, 16),))
    w_out = noise(key_of[4], (H * DV, D), (H * DV) ** -0.5, 0.046875, ((0, 16), (1, 16)))
    latent_cache = draw_latent_cache(jax.random.fold_in(key_of[7], 71), 0)
    lengths = draw_lengths(jax.random.fold_in(key_of[7], 71), 0)
    return dict(q_nope=q_nope, q_rope=q_rope, w_uk=w_uk, w_uv=w_uv, w_out=w_out, latent_cache=latent_cache, lengths=lengths)


def reference(q_nope, q_rope, w_uk, w_uv, w_out, latent_cache, lengths):
    softmax_scale = 1.0 / math.sqrt(DN + R)
    q_latent = jnp.einsum('bhn,hnl->bhl', q_nope.astype(jnp.float32), w_uk.astype(jnp.float32)).astype(jnp.bfloat16)

    def attend(inputs):
        latent_query, rope_query, cache_rows, length = inputs
        scores = jnp.dot(latent_query, cache_rows[:, :LAT].T, preferred_element_type=jnp.float32)
        scores = scores + jnp.dot(rope_query, cache_rows[:, LAT:].T, preferred_element_type=jnp.float32)
        scores = scores * softmax_scale
        is_live = (jnp.arange(CTX, dtype=jnp.int32) < length)[None, :]
        masked = jnp.where(is_live, scores, -1e+30)
        highest = lax.optimization_barrier(jnp.max(masked, axis=1, keepdims=True))
        exponent = jnp.where(is_live, jnp.exp(masked - highest), 0.0)
        weights = (exponent / lax.optimization_barrier(jnp.sum(exponent, axis=1, keepdims=True))).astype(jnp.bfloat16)
        return jnp.dot(weights, cache_rows[:, :LAT], preferred_element_type=jnp.float32)
    latent_out = lax.map(attend, (q_latent, q_rope, latent_cache, lengths)).astype(jnp.bfloat16)
    head_out = jnp.einsum('bhl,hlv->bhv', latent_out.astype(jnp.float32), w_uv.astype(jnp.float32)).astype(jnp.bfloat16)
    merged_heads = head_out.reshape(B, H * DV)
    return jnp.dot(merged_heads, w_out, preferred_element_type=jnp.float32).astype(jnp.bfloat16)
```

```python
import functools
import math

import jax
import jax.numpy as jnp
from jax import lax
from jax.experimental import pallas as pl
from jax.experimental.pallas import tpu as pltpu
from jax.sharding import PartitionSpec as P

MESH = pl.DeviceIdType.MESH
F32 = jnp.float32
BF16 = jnp.bfloat16
FLOOR = -(2.0**90)


def far_first(n):
    return sorted(range(1, n), key=lambda d: -min(d, n - d))


def near_first(n):
    return sorted(range(1, n), key=lambda d: min(d, n - d))


def columns(shape, values):
    lane = lax.broadcasted_iota(jnp.int32, shape, 1)
    out = jnp.zeros(shape, F32)
    for at, value in enumerate(values):
        out = jnp.where(lane == at, value, out)
    return out


def spread(rows, heads):
    count, width = rows.shape
    wide = jnp.concatenate([rows.astype(F32)] * heads, axis=1)
    row_head = lax.rem(lax.broadcasted_iota(jnp.int32, wide.shape, 0), heads)
    col_head = lax.div(lax.broadcasted_iota(jnp.int32, wide.shape, 1), width)
    return jnp.where(row_head == col_head, wide, 0.0).astype(BF16)


def dot_nt(a, b):
    return lax.dot_general(a, b, (((1,), (1,)), ((), ())), preferred_element_type=F32)


def kernel(
    nz,
    ndp,
    scale2,
    lengths,
    qn_hbm,
    qr_hbm,
    wuk_hbm,
    wuv_hbm,
    wout_hbm,
    cache_hbm,
    out_ref,
    qn,
    qr,
    wuk,
    wuv,
    wout,
    cache,
    q0,
    q1,
    qfull,
    scores,
    probs,
    acc_mine,
    acc_other,
    st_mine,
    st_other,
    o_send,
    o_recv,
    heads_buf,
    heads_f32,
    sums_f32,
    sums_send,
    sums_recv,
    out_f32,
    load_sem,
    cache_sem,
    q_ss,
    q_rs,
    f_ss,
    f_rs,
    p_ss,
    p_rs,
    o_ss,
    o_rs,
    h_ss,
    h_rs,
    t_ss,
    t_rs,
):
    nctx = 2 * nz
    i = lax.axis_index("dp")
    c = lax.axis_index("ctx")
    z = lax.div(c, 2)
    k = lax.rem(c, 2)
    other = 1 - k
    seqs, width, span = cache.shape
    lat = wuk.shape[1]
    rope = width - lat
    heads = wuk.shape[0] // qn.shape[1]

    def z_at(d):
        return lax.rem(z + d, nz)

    def z_peer(d):
        return (i, z_at(d) * 2 + k)

    partner = (i, z * 2 + other)

    def ctx_at(d):
        return lax.rem(c + d, nctx)

    def dp_at(d):
        return lax.rem(i + d, ndp)

    loads = [
        pltpu.make_async_copy(src, dst, load_sem.at[n])
        for n, (src, dst) in enumerate(
            ((qn_hbm, qn), (wuk_hbm, wuk), (qr_hbm, qr), (wuv_hbm, wuv), (wout_hbm, wout))
        )
    ]
    for load in loads[:3]:
        load.start()

    barrier = pltpu.get_barrier_semaphore()
    for d in far_first(nctx):
        pl.semaphore_signal(barrier, inc=1, device_id=(i, ctx_at(d)), device_id_type=MESH)
    for d in far_first(ndp):
        pl.semaphore_signal(barrier, inc=1, device_id=(dp_at(d), c), device_id_type=MESH)

    cache_loads = [
        pltpu.make_async_copy(cache_hbm.at[s], cache.at[s], cache_sem.at[s]) for s in range(seqs)
    ]
    for load in cache_loads:
        load.start()
    for load in loads[3:]:
        load.start()

    for load in loads[:3]:
        load.wait()
    q_lat = jnp.dot(spread(qn[...], heads), wuk[...], preferred_element_type=F32)
    half = q_lat.shape[0] // 2
    q0[k, z, :, :lat] = q_lat[:half].astype(BF16)
    q1[k, z] = q_lat[half:].astype(BF16)
    rope_rows = qr[...].astype(F32)
    q0[k, z, :, lat:] = jnp.concatenate([rope_rows[:half], rope_rows[half:]], axis=1).astype(BF16)

    pl.semaphore_wait(barrier, nctx + ndp - 2)

    q_bufs = (q0, q1)

    def remote(src, dst, ss, rs, device):
        return pltpu.make_async_remote_copy(
            src_ref=src, dst_ref=dst, send_sem=ss, recv_sem=rs, device_id=device, device_id_type=MESH
        )

    sent = []

    def send(*args):
        copy = remote(*args)
        copy.start()
        sent.append(copy)

    for a, buf in enumerate(q_bufs):
        own = buf.at[k, z]
        for d in far_first(nz):
            send(own, own, q_ss.at[a, d], q_rs.at[a, d], z_peer(d))
        send(own, own, f_ss.at[a, 0], f_rs.at[a, 0], partner)

    def forward(a):
        buf = q_bufs[a]
        for d in near_first(nz):
            slot = buf.at[k, z_at(nz - d)]
            remote(slot, slot, q_ss.at[a, d], q_rs.at[a, d], z_peer(d)).wait_recv()
            send(slot, slot, f_ss.at[a, d], f_rs.at[a, d], partner)

    def gathered(a):
        buf = q_bufs[a]
        for d in [0] + near_first(nz):
            slot = buf.at[other, z_at(nz - d) if d else z]
            remote(slot, slot, f_ss.at[a, d], f_rs.at[a, d], partner).wait_recv()

    block = min(512, span)

    def rows_of(buf, u, start, stop):
        rows = buf[:, :, :, start:stop].astype(F32)
        rows = rows.reshape(nctx, 2, heads, stop - start)
        return rows[:, u].reshape(nctx * heads, stop - start)

    def attend(a):
        stats = []
        for u in range(2):
            s = 2 * a + u
            cache_loads[s].wait()
            qfull[:, :lat] = rows_of(q_bufs[a], u, 0, lat).astype(BF16)
            ropes = rows_of(q0, u, lat, lat + 2 * rope)
            qfull[:, lat:] = ropes[:, a * rope : (a + 1) * rope].astype(BF16)
            top = jnp.full((nctx * heads, 128), -1e30, F32)
            live = lengths[s] - c * span
            for b in range(span // block):
                part = jnp.dot(
                    qfull[...],
                    cache[s, :, b * block : (b + 1) * block],
                    preferred_element_type=F32,
                )
                position = b * block + lax.broadcasted_iota(jnp.int32, part.shape, 1)
                part = jnp.where(position < live, part, -1e30)
                scores[:, b * block : (b + 1) * block] = part
                for e in range(block // 128):
                    top = jnp.maximum(top, part[:, e * 128 : (e + 1) * 128])
            m2 = jnp.maximum(jnp.max(top, axis=1, keepdims=True) * scale2, FLOOR)
            total = jnp.zeros((nctx * heads, 128), F32)
            for b in range(span // block):
                part = jnp.exp2(scores[:, b * block : (b + 1) * block] * scale2 - m2)
                probs[:, b * block : (b + 1) * block] = part.astype(BF16)
                for e in range(block // 128):
                    total = total + part[:, e * 128 : (e + 1) * 128]
            stats += [m2, jnp.sum(total, axis=1, keepdims=True)]
            acc = dot_nt(probs[...], cache[s, :lat, :]).astype(BF16)
            mid = nz * heads
            acc_mine[a, 0, u] = acc[:mid]
            acc_mine[a, 1, u] = acc[mid:]
        table = columns((nctx * heads, 128), stats)
        st_mine[a, 0] = table[: nz * heads]
        st_mine[a, 1] = table[nz * heads :]
        send(acc_mine.at[a, other], acc_other.at[a], p_ss.at[a, 0], p_rs.at[a, 0], partner)
        send(st_mine.at[a, other], st_other.at[a], p_ss.at[a, 1], p_rs.at[a, 1], partner)

    def exchange(a):
        remote(
            acc_mine.at[a, other], acc_other.at[a], p_ss.at[a, 0], p_rs.at[a, 0], partner
        ).wait_recv()
        remote(
            st_mine.at[a, other], st_other.at[a], p_ss.at[a, 1], p_rs.at[a, 1], partner
        ).wait_recv()
        mine, theirs = st_mine[a, k], st_other[a]
        data, stats = [], []
        for u in range(2):
            m_a, l_a = mine[:, 2 * u : 2 * u + 1], mine[:, 2 * u + 1 : 2 * u + 2]
            m_b, l_b = theirs[:, 2 * u : 2 * u + 1], theirs[:, 2 * u + 1 : 2 * u + 2]
            m = jnp.maximum(m_a, m_b)
            m_hi = m.astype(BF16).astype(F32)
            m_lo = (m - m_hi).astype(BF16).astype(F32)
            m = m_hi + m_lo
            w_a, w_b = jnp.exp2(m_a - m), jnp.exp2(m_b - m)
            l = w_a * l_a + w_b * l_b
            l_hi = l.astype(BF16).astype(F32)
            l_lo = l - l_hi
            joined = w_a * acc_mine[a, k, u].astype(F32) + w_b * acc_other[a, u].astype(F32)
            data.append(joined.reshape(nz, 1, heads, lat))
            table = columns((nz * heads, 128), (m_hi, m_lo, l_hi, l_lo))
            stats.append(table.reshape(nz, 1, heads, 128))
        data = jnp.concatenate(data, axis=1).reshape(nz, 2 * heads, lat)
        stats = jnp.concatenate(stats, axis=1).reshape(nz, 2 * heads, 128)
        o_send[a, :, :, :lat] = data.astype(BF16)
        o_send[a, :, :, lat:] = stats.astype(BF16)
        for d in far_first(nz):
            send(o_send.at[a, z_at(d)], o_recv.at[a, z], o_ss.at[a, d], o_rs.at[a, d], z_peer(d))
        o_recv[a, z] = o_send[a, z]

    def finish(a):
        for d in near_first(nz):
            came = z_at(nz - d)
            remote(
                o_send.at[a, came], o_recv.at[a, came], o_ss.at[a, d], o_rs.at[a, d], z_peer(d)
            ).wait_recv()
        tops, sums = [], []
        for n in range(nz):
            table = o_recv[a, n, :, lat:].astype(F32)
            tops.append(table[:, 0:1] + table[:, 1:2])
            sums.append(table[:, 2:3] + table[:, 3:4])
        top = functools.reduce(jnp.maximum, tops)
        numerator = jnp.zeros((2 * heads, lat), F32)
        denominator = jnp.zeros((2 * heads, 1), F32)
        for n in range(nz):
            w = jnp.exp2(tops[n] - top)
            denominator = denominator + w * sums[n]
            numerator = numerator + w * o_recv[a, n, :, :lat].astype(F32)
        return numerator / denominator

    forward(0)
    gathered(0)
    attend(0)
    forward(1)
    exchange(0)
    gathered(1)
    attend(1)
    exchange(1)
    latents = jnp.concatenate([finish(0), finish(1)], axis=0).astype(BF16)

    loads[3].wait()
    head_out = jnp.dot(spread(latents, heads), wuv[...], preferred_element_type=F32)
    heads_buf[i] = head_out.astype(BF16)
    for d in far_first(ndp):
        own = heads_buf.at[i]
        send(own, own, h_ss.at[d], h_rs.at[d], (dp_at(d), c))
    loads[4].wait()
    for d in near_first(ndp):
        slot = heads_buf.at[dp_at(ndp - d)]
        remote(slot, slot, h_ss.at[d], h_rs.at[d], (dp_at(d), c)).wait_recv()
    heads_f32[...] = heads_buf[...].astype(F32).reshape(heads_f32.shape)
    rows = ndp * seqs
    merged = jnp.concatenate(
        [heads_f32[pl.ds(h, rows, stride=heads), :] for h in range(heads)], axis=1
    ).astype(BF16)
    terms = dot_nt(merged, wout[...])
    cols = terms.shape[1]
    pieces = -(-cols // 128)
    for n in range(pieces):
        piece = terms[:, n * 128 : min(cols, (n + 1) * 128)]
        if piece.shape[1] < 128:
            piece = jnp.concatenate(
                [piece, jnp.zeros((rows, 128 - piece.shape[1]), F32)], axis=1
            )
        sums_f32[pl.ds(n, rows, stride=pieces), :] = piece
    sums_send[...] = sums_f32[...].astype(BF16).reshape(sums_send.shape)
    for d in far_first(nctx):
        send(
            sums_send.at[ctx_at(d)], sums_recv.at[c], t_ss.at[d], t_rs.at[d], (i, ctx_at(d))
        )
    sums_recv[c] = sums_send[c]
    for d in near_first(nctx):
        came = ctx_at(nctx - d)
        remote(
            sums_send.at[came], sums_recv.at[came], t_ss.at[d], t_rs.at[d], (i, ctx_at(d))
        ).wait_recv()
    out_f32[...] = jnp.sum(sums_recv[...].astype(F32), axis=0)
    out_rows = out_ref.shape[0]
    for n in range(pieces):
        end = min(cols, (n + 1) * 128)
        piece = out_f32[pl.ds(n, out_rows, stride=pieces), :]
        out_ref[:, n * 128 : end] = piece[:, : end - n * 128].astype(BF16)
    for copy in sent:
        copy.wait_send()


def per_device(nz, ndp, q_nope, q_rope, w_uk, w_uv, w_out, latent_cache, lengths):
    seqs, heads, dn = q_nope.shape
    rope = q_rope.shape[2]
    lat = w_uk.shape[2]
    span = latent_cache.shape[1]
    dv = w_uv.shape[2]
    cols = w_out.shape[1]
    nctx = 2 * nz
    every = nctx * heads
    pieces = -(-cols // 128)
    out_rows = ndp * seqs // nctx
    scale2 = math.log2(math.e) / math.sqrt(dn + rope)
    vmem, dma = pltpu.VMEM, pltpu.SemaphoreType.DMA
    hbm = pl.BlockSpec(memory_space=pltpu.HBM)
    return pl.pallas_call(
        functools.partial(kernel, nz, ndp, scale2),
        out_shape=jax.ShapeDtypeStruct((out_rows, cols), BF16),
        in_specs=[pl.BlockSpec(memory_space=pltpu.SMEM)] + [hbm] * 6,
        out_specs=pl.BlockSpec(memory_space=vmem),
        scratch_shapes=[
            vmem((seqs * heads, dn), BF16),
            vmem((seqs * heads, rope), BF16),
            vmem((heads * dn, lat), BF16),
            vmem((heads * lat, dv), BF16),
            vmem((cols, heads * dv), BF16),
            vmem((seqs, lat + rope, span), BF16),
            vmem((2, nz, 2 * heads, lat + 2 * rope), BF16),
            vmem((2, nz, 2 * heads, lat), BF16),
            vmem((every, lat + rope), BF16),
            vmem((every, span), F32),
            vmem((every, span), BF16),
            vmem((2, 2, 2, nz * heads, lat), BF16),
            vmem((2, 2, nz * heads, lat), BF16),
            vmem((2, 2, nz * heads, 128), F32),
            vmem((2, nz * heads, 128), F32),
            vmem((2, nz, 2 * heads, lat + 128), BF16),
            vmem((2, nz, 2 * heads, lat + 128), BF16),
            vmem((ndp, seqs * heads, dv), BF16),
            vmem((ndp * seqs * heads, dv), F32),
            vmem((ndp * seqs * pieces, 128), F32),
            vmem((nctx, out_rows * pieces, 128), BF16),
            vmem((nctx, out_rows * pieces, 128), BF16),
            vmem((out_rows * pieces, 128), F32),
            dma((5,)),
            dma((seqs,)),
            dma((2, nz)),
            dma((2, nz)),
            dma((2, nz)),
            dma((2, nz)),
            dma((2, 2)),
            dma((2, 2)),
            dma((2, nz)),
            dma((2, nz)),
            dma((ndp,)),
            dma((ndp,)),
            dma((nctx,)),
            dma((nctx,)),
        ],
        compiler_params=pltpu.CompilerParams(
            collective_id=0, has_side_effects=True, vmem_limit_bytes=60 << 20
        ),
        name="mla_decode",
    )(
        lengths,
        q_nope.reshape(seqs * heads, dn),
        q_rope.reshape(seqs * heads, rope),
        w_uk.reshape(heads * dn, lat),
        w_uv.reshape(heads * lat, dv),
        w_out.T,
        jnp.swapaxes(latent_cache, 1, 2),
    )


def solution(mesh):
    in_specs = (
        P("dp", "ctx", None),
        P("dp", "ctx", None),
        P("ctx", None, None),
        P("ctx", None, None),
        P("ctx", "dp"),
        P("dp", "ctx", None),
        P("dp"),
    )
    out_specs = P("ctx", "dp")
    return jax.shard_map(
        functools.partial(per_device, mesh.shape["ctx"] // 2, mesh.shape["dp"]),
        mesh=mesh,
        in_specs=in_specs,
        out_specs=out_specs,
        check_vma=False,
    )
```

```python
import functools
import math

import jax
import jax.numpy as jnp
from jax import lax
from jax.experimental import pallas as pl
from jax.experimental.pallas import tpu as pltpu
from jax.sharding import PartitionSpec as P

MESH = pl.DeviceIdType.MESH
F32 = jnp.float32
BF16 = jnp.bfloat16
FLOOR = -(2.0**90)


def far_first(n, size):
    step = lax.div(n + 1, 2)
    return size // 2 + jnp.where(lax.rem(n, 2) == 1, -step, step)


def near_first(n, size):
    return far_first(size - 2 - n, size)


AWAY = (0, 1, 7, 2, 6, 3, 5, 4)


def loop(count, body):
    lax.fori_loop(0, count, lambda n, carry: (body(n), carry)[1], 0)


def columns(shape, values):
    lane = lax.broadcasted_iota(jnp.int32, shape, 1)
    out = jnp.zeros(shape, F32)
    for at, value in values:
        out = jnp.where(lane == at, value, out)
    return out


def spread(rows, heads):
    count, width = rows.shape
    wide = jnp.concatenate([rows.astype(F32)] * heads, axis=1)
    row_head = lax.rem(lax.broadcasted_iota(jnp.int32, wide.shape, 0), heads)
    col_head = lax.div(lax.broadcasted_iota(jnp.int32, wide.shape, 1), width)
    return jnp.where(row_head == col_head, wide, 0.0).astype(BF16)


def dot_nt(a, b):
    return lax.dot_general(a, b, (((1,), (1,)), ((), ())), preferred_element_type=F32)


def remote(src, dst, ss, rs, device):
    return pltpu.make_async_remote_copy(
        src_ref=src, dst_ref=dst, send_sem=ss, recv_sem=rs, device_id=device, device_id_type=MESH
    )


def kernel(
    nz,
    ndp,
    scale2,
    len_hbm,
    qn_hbm,
    qr_hbm,
    wuk_hbm,
    wuv_hbm,
    wout_hbm,
    cache_hbm,
    out_ref,
    lengths,
    qn,
    qr,
    wuk,
    wuv,
    wout,
    cache,
    values,
    q_buf,
    r_buf,
    qfull,
    scores,
    probs,
    st_mine,
    st_other,
    acc_mine,
    acc_other,
    zs_send,
    zs_recv,
    o_send,
    o_recv,
    latents,
    heads_buf,
    heads_f32,
    sums_f32,
    sums_send,
    sums_recv,
    out_f32,
    load_sem,
    cache_sem,
    q_ss,
    q_rs,
    f_ss,
    f_rs,
    p_ss,
    p_rs,
    s_ss,
    s_rs,
    o_ss,
    o_rs,
    h_ss,
    h_rs,
    t_ss,
    t_rs,
):
    nctx = 2 * nz
    i = lax.axis_index("dp")
    c = lax.axis_index("ctx")
    z = lax.div(c, 2)
    k = lax.rem(c, 2)
    other = 1 - k
    seqs, width, span = cache.shape
    lat = wuk.shape[1]
    rope = width - lat
    heads = wuk.shape[0] // qn.shape[1]
    every = nctx * heads
    half = lat // 2

    def z_at(d):
        return lax.rem(z + d, nz)

    def z_peer(d):
        return (i, z_at(d) * 2 + k)

    partner = (i, z * 2 + other)

    def ctx_at(d):
        return lax.rem(c + d, nctx)

    def dp_at(d):
        return lax.rem(i + d, ndp)

    loads = [
        pltpu.make_async_copy(src, dst, load_sem.at[n])
        for n, (src, dst) in enumerate(
            (
                (wuk_hbm, wuk),
                (qn_hbm, qn),
                (qr_hbm, qr),
                (len_hbm, lengths),
                (wuv_hbm, wuv),
                (wout_hbm, wout),
            )
        )
    ]

    def cache_load(s):
        return pltpu.make_async_copy(cache_hbm.at[s], cache.at[s], cache_sem.at[s])

    loads[0].start()
    loads[1].start()

    barrier = pltpu.get_barrier_semaphore()

    def greet(peer):
        pl.semaphore_signal(barrier, inc=1, device_id=peer, device_id_type=MESH)

    for slot in range(nz - 1, 0, -1):
        greet(z_peer(AWAY[slot]))
    greet(partner)
    for d in range(1, ndp):
        greet((dp_at(d), c))

    loads[2].start()
    loads[3].start()
    loop(seqs, lambda s: cache_load(s).start())
    loads[4].start()
    loads[5].start()

    loads[2].wait()
    rows = qr[...].astype(F32)
    mid = seqs * heads // 2
    r_buf[k, 0] = jnp.concatenate([rows[:mid], rows[mid:]], axis=1).astype(BF16)

    loads[0].wait()
    loads[1].wait()
    q_lat = jnp.dot(spread(qn[...], heads), wuk[...], preferred_element_type=F32)
    for s in range(seqs):
        rows = q_lat[s * heads : (s + 1) * heads]
        q_buf[s, k, 0] = jnp.concatenate([rows[:, :half], rows[:, half:]], axis=0).astype(BF16)

    pl.semaphore_wait(barrier, nz + ndp - 1)

    def block_of(s, core, slot):
        return r_buf.at[core, slot] if isinstance(s, int) and s == seqs else q_buf.at[s, core, slot]

    def give(s, slot):
        return remote(
            block_of(s, k, 0),
            block_of(s, k, slot),
            q_ss.at[s, slot],
            q_rs.at[s, slot],
            z_peer(AWAY[slot]),
        )

    def hand(s, core):
        ref = r_buf.at[core] if isinstance(s, int) and s == seqs else q_buf.at[s, core]
        return remote(ref, ref, f_ss.at[s], f_rs.at[s], partner)

    order = (seqs,) + tuple(range(seqs))
    for s in order:
        for slot in range(nz - 1, 0, -1):
            give(s, slot).start()

    def pass_over(s):
        for slot in range(1, nz):
            give(s, slot).wait_recv()
        hand(s, k).start()

    def turn(s):
        cache_load(s).wait()
        for b in range(span // 256):
            part = cache[s, :lat, b * 256 : (b + 1) * 256]
            values[s, b * 256 : (b + 1) * 256, :] = part.T

    loop(seqs, turn)

    def st_copy(s):
        return remote(
            st_mine.at[s, other], st_other.at[s], p_ss.at[s, 0], p_rs.at[s, 0], partner
        )

    def acc_copy(s):
        return remote(
            acc_mine.at[s, other], acc_other.at[s], p_ss.at[s, 1], p_rs.at[s, 1], partner
        )

    def o_copy(s, slot):
        return remote(
            o_send.at[s, slot],
            o_recv.at[s, slot],
            o_ss.at[s, slot],
            o_rs.at[s, slot],
            z_peer((nz - AWAY[slot]) % nz),
        )

    def zs_copy(slot):
        return remote(
            zs_send.at[slot],
            zs_recv.at[slot],
            s_ss.at[slot],
            s_rs.at[slot],
            z_peer((nz - AWAY[slot]) % nz),
        )

    block = min(512, span)
    blocks = span // block

    def attend(s):
        for e in range(2):
            rows = q_buf[s, :, :, e * heads : (e + 1) * heads, :].astype(F32)
            qfull[:, e * half : (e + 1) * half] = rows.reshape(every, half).astype(BF16)
        ropes = r_buf[...].astype(F32).reshape(nctx, 2, heads, 2 * rope)
        odd = lax.rem(s, 2) == 1
        ropes = jnp.where(odd, ropes[:, 1], ropes[:, 0]).reshape(every, 2 * rope)
        late = s >= seqs // 2
        qfull[:, lat:] = jnp.where(late, ropes[:, rope:], ropes[:, :rope]).astype(BF16)
        top = jnp.full((every, 128), -1e30, F32)
        live = lengths[s] - c * span
        for b in range(blocks):
            part = jnp.dot(
                qfull[...],
                cache[s, :, b * block : (b + 1) * block],
                preferred_element_type=F32,
            )
            position = b * block + lax.broadcasted_iota(jnp.int32, part.shape, 1)
            part = jnp.where(position < live, part, -1e30)
            scores[:, b * block : (b + 1) * block] = part
            for e in range(block // 128):
                top = jnp.maximum(top, part[:, e * 128 : (e + 1) * 128])
        m2 = jnp.maximum(jnp.max(top, axis=1, keepdims=True) * scale2, FLOOR)
        total = jnp.zeros((every, 128), F32)
        for b in range(blocks):
            part = jnp.exp2(scores[:, b * block : (b + 1) * block] * scale2 - m2)
            probs[:, b * block : (b + 1) * block] = part.astype(BF16)
            for e in range(block // 128):
                total = total + part[:, e * 128 : (e + 1) * 128]
        l = jnp.sum(total, axis=1, keepdims=True)
        table = columns((every, 128), ((0, m2), (1, l)))
        st_mine[s, 0] = table[: every // 2]
        st_mine[s, 1] = table[every // 2 :]
        st_copy(s).start()
        acc = jnp.dot(probs[...], values[s], preferred_element_type=F32).astype(BF16)
        acc_mine[s, 0] = acc[: every // 2]
        acc_mine[s, 1] = acc[every // 2 :]
        acc_copy(s).start()

    def combine(s, last):
        st_copy(s).wait_recv()
        mine, theirs = st_mine[s, k], st_other[s]
        m_a, l_a = mine[:, 0:1], mine[:, 1:2]
        m_b, l_b = theirs[:, 0:1], theirs[:, 1:2]
        m = jnp.maximum(m_a, m_b)
        w_a, w_b = jnp.exp2(m_a - m), jnp.exp2(m_b - m)
        l = w_a * l_a + w_b * l_b
        table = columns((nz * heads, 128), ((2 * s, m), (2 * s + 1, l))).reshape(nz, heads, 128)
        if last:
            zs_send[...] += table

            for slot in range(nz - 1, 0, -1):
                zs_copy(slot).start()
            zs_recv[0] = zs_send[0]
        else:
            zs_send[...] += table
        acc_copy(s).wait_recv()
        joined = w_a * acc_mine[s, k].astype(F32) + w_b * acc_other[s].astype(F32)
        joined = joined.reshape(nz, heads, lat)
        joined = jnp.concatenate([joined[:, :, :half], joined[:, :, half:]], axis=1)
        o_send[s] = joined.astype(BF16)

        for slot in range(nz - 1, 0, -1):
            o_copy(s, slot).start()
        o_recv[s, 0] = o_send[s, 0]

    zs_send[...] = jnp.zeros_like(zs_send)
    pass_over(seqs)
    pass_over(0)
    hand(seqs, other).wait_recv()
    loads[3].wait()

    def step(s):
        @pl.when(s + 1 < seqs)
        def _():
            pass_over(s + 1)

        hand(s, other).wait_recv()
        attend(s)

        @pl.when(s > 0)
        def _():
            combine(s - 1, False)

    loop(seqs, step)
    combine(seqs - 1, True)

    def h_copy(p, d, slot):
        ref = heads_buf.at[p, slot]
        return remote(ref, ref, h_ss.at[p, d], h_rs.at[p, d], (dp_at(d), c))

    loads[4].wait()

    for slot in range(1, nz):
        zs_copy(slot).wait_recv()

    def finish(s, row):
        for slot in range(1, nz):
            o_copy(s, slot).wait_recv()
        lane = lax.broadcasted_iota(jnp.int32, (nz, heads, 128), 2)
        table = zs_recv[...]
        m = jnp.sum(jnp.where(lane == 2 * s, table, 0.0), axis=2, keepdims=True)
        l = jnp.sum(jnp.where(lane == 2 * s + 1, table, 0.0), axis=2, keepdims=True)
        top = jnp.max(m, axis=0, keepdims=True)
        w = jnp.exp2(m - top)
        w = w / jnp.sum(w * l, axis=0, keepdims=True)
        data = o_recv[s].astype(F32)
        left = jnp.sum(w * data[:, :heads], axis=0)
        right = jnp.sum(w * data[:, heads:], axis=0)
        latents[pl.ds(row, heads), :] = jnp.concatenate([left, right], axis=1)

    def project(p):
        for e in range(seqs // 2):
            finish(p * (seqs // 2) + e, e * heads)
        head_out = jnp.dot(
            spread(latents[...].astype(BF16), heads), wuv[...], preferred_element_type=F32
        )
        heads_buf[p, i] = head_out.astype(BF16)

        def give(n):
            h_copy(p, far_first(n, ndp), i).start()

        loop(ndp - 1, give)

    loop(2, project)
    loads[5].wait()

    def heads_arrive(n):
        p = lax.div(n, ndp - 1)
        d = near_first(lax.rem(n, ndp - 1), ndp)
        h_copy(p, d, dp_at(ndp - d)).wait_recv()

    loop(2 * (ndp - 1), heads_arrive)
    heads_f32[...] = heads_buf[...].astype(F32).reshape(heads_f32.shape)
    rows = ndp * seqs
    merged = jnp.concatenate(
        [heads_f32[pl.ds(h, rows, stride=heads), :] for h in range(heads)], axis=1
    ).astype(BF16)
    terms = dot_nt(merged, wout[...])
    cols = terms.shape[1]
    pieces = -(-cols // 128)
    for p in range(2):
        for n in range(pieces):
            piece = terms[p * rows // 2 : (p + 1) * rows // 2, n * 128 : min(cols, (n + 1) * 128)]
            if piece.shape[1] < 128:
                piece = jnp.concatenate(
                    [piece, jnp.zeros((rows // 2, 128 - piece.shape[1]), F32)], axis=1
                )
            sums_f32[pl.ds(p * pieces + n, rows // 2, stride=2 * pieces), :] = piece
    sums_send[...] = sums_f32[...].astype(BF16).reshape(sums_send.shape)

    def t_copy(d, at, slot):
        return remote(
            sums_send.at[at], sums_recv.at[slot], t_ss.at[d], t_rs.at[d], (i, ctx_at(d))
        )

    def t_start(n):
        d = far_first(n, nctx)
        t_copy(d, ctx_at(d), c).start()

    loop(nctx - 1, t_start)
    sums_recv[c] = sums_send[c]

    for slot in range(1, nz):
        zs_copy(slot).wait_send()
        give(seqs, slot).wait_send()
    hand(seqs, k).wait_send()

    def sent(s):
        hand(s, k).wait_send()
        for slot in range(1, nz):
            give(s, slot).wait_send()
        st_copy(s).wait_send()
        acc_copy(s).wait_send()
        for slot in range(1, nz):
            o_copy(s, slot).wait_send()

    loop(seqs, sent)

    def sent_heads(n):
        h_copy(0, n + 1, i).wait_send()
        h_copy(1, n + 1, i).wait_send()

    loop(ndp - 1, sent_heads)

    def sums_arrive(n):
        d = near_first(n, nctx)
        came = ctx_at(nctx - d)
        t_copy(d, came, came).wait_recv()

    loop(nctx - 1, sums_arrive)
    out_f32[...] = jnp.sum(sums_recv[...].astype(F32), axis=0)
    for p in range(2):
        for n in range(pieces):
            end = min(cols, (n + 1) * 128)
            piece = out_f32[pl.ds(p * pieces + n, seqs // 2, stride=2 * pieces), :]
            out_ref[p * seqs // 2 : (p + 1) * seqs // 2, n * 128 : end] = piece[
                :, : end - n * 128
            ].astype(BF16)

    loop(nctx - 1, lambda n: t_copy(n + 1, ctx_at(n + 1), c).wait_send())


def per_device(nz, ndp, q_nope, q_rope, w_uk, w_uv, w_out, latent_cache, lengths):
    seqs, heads, dn = q_nope.shape
    rope = q_rope.shape[2]
    lat = w_uk.shape[2]
    span = latent_cache.shape[1]
    dv = w_uv.shape[2]
    cols = w_out.shape[1]
    nctx = 2 * nz
    every = nctx * heads
    own = nz * heads
    pieces = -(-cols // 128)
    scale2 = math.log2(math.e) / math.sqrt(dn + rope)
    vmem, dma = pltpu.VMEM, pltpu.SemaphoreType.DMA
    hbm = pl.BlockSpec(memory_space=pltpu.HBM)
    return pl.pallas_call(
        functools.partial(kernel, nz, ndp, scale2),
        out_shape=jax.ShapeDtypeStruct((seqs, cols), BF16),
        in_specs=[hbm] * 7,
        out_specs=pl.BlockSpec(memory_space=vmem),
        scratch_shapes=[
            pltpu.SMEM((seqs,), jnp.int32),
            vmem((seqs * heads, dn), BF16),
            vmem((seqs * heads, rope), BF16),
            vmem((heads * dn, lat), BF16),
            vmem((heads * lat, dv), BF16),
            vmem((cols, heads * dv), BF16),
            vmem((seqs, lat + rope, span), BF16),
            vmem((seqs, span, lat), BF16),
            vmem((seqs, 2, nz, 2 * heads, lat // 2), BF16),
            vmem((2, nz, 2 * heads, 2 * rope), BF16),
            vmem((every, lat + rope), BF16),
            vmem((every, span), F32),
            vmem((every, span), BF16),
            vmem((seqs, 2, own, 128), F32),
            vmem((seqs, own, 128), F32),
            vmem((seqs, 2, own, lat), BF16),
            vmem((seqs, own, lat), BF16),
            vmem((nz, heads, 128), F32),
            vmem((nz, heads, 128), F32),
            vmem((seqs, nz, 2 * heads, lat // 2), BF16),
            vmem((seqs, nz, 2 * heads, lat // 2), BF16),
            vmem((seqs // 2 * heads, lat), F32),
            vmem((2, ndp, seqs // 2 * heads, dv), BF16),
            vmem((ndp * seqs * heads, dv), F32),
            vmem((ndp * seqs * pieces, 128), F32),
            vmem((nctx, seqs * pieces, 128), BF16),
            vmem((nctx, seqs * pieces, 128), BF16),
            vmem((seqs * pieces, 128), F32),
            dma((6,)),
            dma((seqs,)),
            dma((seqs + 1, nz)),
            dma((seqs + 1, nz)),
            dma((seqs + 1,)),
            dma((seqs + 1,)),
            dma((seqs, 2)),
            dma((seqs, 2)),
            dma((nz,)),
            dma((nz,)),
            dma((seqs, nz)),
            dma((seqs, nz)),
            dma((2, ndp)),
            dma((2, ndp)),
            dma((nctx,)),
            dma((nctx,)),
        ],
        compiler_params=pltpu.CompilerParams(
            collective_id=0, has_side_effects=True, vmem_limit_bytes=60 << 20
        ),
        name="mla_decode",
    )(
        lengths,
        q_nope.reshape(seqs * heads, dn),
        q_rope.reshape(seqs * heads, rope),
        w_uk.reshape(heads * dn, lat),
        w_uv.reshape(heads * lat, dv),
        w_out.T,
        jnp.swapaxes(latent_cache, 1, 2),
    )


def solution(mesh):
    in_specs = (
        P("dp", "ctx", None),
        P("dp", "ctx", None),
        P("ctx", None, None),
        P("ctx", None, None),
        P("ctx", "dp"),
        P("dp", "ctx", None),
        P("dp"),
    )
    out_specs = P("ctx", "dp")
    return jax.shard_map(
        functools.partial(per_device, mesh.shape["ctx"] // 2, mesh.shape["dp"]),
        mesh=mesh,
        in_specs=in_specs,
        out_specs=out_specs,
        check_vma=False,
    )
```

```python
import functools
import math

import jax
import jax.numpy as jnp
from jax import lax
from jax.experimental import pallas as pl
from jax.experimental.pallas import tpu as pltpu
from jax.sharding import PartitionSpec as P

MESH = pl.DeviceIdType.MESH
F32 = jnp.float32
BF16 = jnp.bfloat16
FLOOR = -(2.0**90)


def far_first(size):
    return sorted(range(1, size), key=lambda d: -min(d, size - d))


def near_first(size):
    return sorted(range(1, size), key=lambda d: min(d, size - d))


AWAY = (0, 1, 7, 2, 6, 3, 5, 4)


def loop(count, body):
    lax.fori_loop(0, count, lambda n, carry: (body(n), carry)[1], 0)


def columns(shape, values):
    lane = lax.broadcasted_iota(jnp.int32, shape, 1)
    out = jnp.zeros(shape, F32)
    for at, value in values:
        out = jnp.where(lane == at, value, out)
    return out


def spread(rows, heads):
    count, width = rows.shape
    wide = jnp.concatenate([rows.astype(F32)] * heads, axis=1)
    row_head = lax.rem(lax.broadcasted_iota(jnp.int32, wide.shape, 0), heads)
    col_head = lax.div(lax.broadcasted_iota(jnp.int32, wide.shape, 1), width)
    return jnp.where(row_head == col_head, wide, 0.0).astype(BF16)


def remote(src, dst, ss, rs, device):
    return pltpu.make_async_remote_copy(
        src_ref=src, dst_ref=dst, send_sem=ss, recv_sem=rs, device_id=device, device_id_type=MESH
    )


def kernel(
    nz,
    ndp,
    scale2,
    len_hbm,
    qn_hbm,
    qr_hbm,
    wuk_hbm,
    wuv_hbm,
    wout_hbm,
    cache_hbm,
    out_ref,
    lengths,
    qn,
    qr,
    wuk,
    wuv,
    wout,
    wout_t,
    cache,
    values,
    q_buf,
    r_buf,
    qfull,
    scores,
    probs,
    st_mine,
    st_other,
    acc_mine,
    acc_other,
    zs_send,
    zs_recv,
    o_send,
    o_recv,
    latents,
    heads_buf,
    heads_f32,
    sums_f32,
    sums_send,
    sums_recv,
    out_f32,
    load_sem,
    cache_sem,
    q_ss,
    q_rs,
    f_ss,
    f_rs,
    p_ss,
    p_rs,
    s_ss,
    s_rs,
    o_ss,
    o_rs,
    h_ss,
    h_rs,
    t_ss,
    t_rs,
):
    nctx = 2 * nz
    i = lax.axis_index("dp")
    c = lax.axis_index("ctx")
    z = lax.div(c, 2)
    k = lax.rem(c, 2)
    other = 1 - k
    seqs, width, span = cache.shape
    lat = wuk.shape[1]
    rope = width - lat
    heads = wuk.shape[0] // qn.shape[1]
    every = nctx * heads
    half = lat // 2

    def z_at(d):
        return lax.rem(z + d, nz)

    def z_peer(d):
        return (i, z_at(d) * 2 + k)

    partner = (i, z * 2 + other)

    def ctx_at(d):
        return lax.rem(c + d, nctx)

    def dp_at(d):
        return lax.rem(i + d, ndp)

    loads = [
        pltpu.make_async_copy(src, dst, load_sem.at[n])
        for n, (src, dst) in enumerate(
            (
                (wuk_hbm, wuk),
                (qn_hbm, qn),
                (qr_hbm, qr),
                (len_hbm, lengths),
                (wuv_hbm, wuv),
                (wout_hbm, wout),
            )
        )
    ]

    def cache_load(s):
        return pltpu.make_async_copy(cache_hbm.at[s], cache.at[s], cache_sem.at[s])

    loads[0].start()
    loads[1].start()

    barrier = pltpu.get_barrier_semaphore()

    def greet(peer):
        pl.semaphore_signal(barrier, inc=1, device_id=peer, device_id_type=MESH)

    for slot in range(nz - 1, 0, -1):
        greet(z_peer(AWAY[slot]))
    greet(partner)
    for d in range(1, ndp):
        greet((dp_at(d), c))

    loads[2].start()
    loads[3].start()
    loop(seqs, lambda s: cache_load(s).start())
    loads[4].start()
    loads[5].start()

    loads[2].wait()
    rows = qr[...].astype(F32)
    mid = seqs * heads // 2
    r_buf[k, 0] = jnp.concatenate([rows[:mid], rows[mid:]], axis=1).astype(BF16)

    loads[0].wait()
    loads[1].wait()
    q_lat = jnp.dot(spread(qn[...], heads), wuk[...], preferred_element_type=F32)
    for s in range(seqs):
        rows = q_lat[s * heads : (s + 1) * heads]
        q_buf[s, k, 0] = jnp.concatenate([rows[:, :half], rows[:, half:]], axis=0).astype(BF16)

    pl.semaphore_wait(barrier, nz + ndp - 1)

    def block_of(s, core, slot):
        return r_buf.at[core, slot] if isinstance(s, int) and s == seqs else q_buf.at[s, core, slot]

    def give(s, slot):
        return remote(
            block_of(s, k, 0),
            block_of(s, k, slot),
            q_ss.at[s, slot],
            q_rs.at[s, slot],
            z_peer(AWAY[slot]),
        )

    def hand(s, core):
        ref = r_buf.at[core] if isinstance(s, int) and s == seqs else q_buf.at[s, core]
        return remote(ref, ref, f_ss.at[s], f_rs.at[s], partner)

    order = (seqs,) + tuple(range(seqs))
    for s in order:
        for slot in range(nz - 1, 0, -1):
            give(s, slot).start()

    def pass_over(s):
        for slot in range(1, nz):
            give(s, slot).wait_recv()
        hand(s, k).start()

    def turn(s):
        cache_load(s).wait()
        for b in range(span // 256):
            part = cache[s, :lat, b * 256 : (b + 1) * 256]
            values[s, b * 256 : (b + 1) * 256, :] = part.T

    loop(seqs, turn)
    loads[5].wait()
    wout_t[...] = wout[...].T

    def st_copy(s):
        return remote(
            st_mine.at[s, other], st_other.at[s], p_ss.at[s, 0], p_rs.at[s, 0], partner
        )

    def acc_copy(s):
        return remote(
            acc_mine.at[s, other], acc_other.at[s], p_ss.at[s, 1], p_rs.at[s, 1], partner
        )

    def o_copy(s, slot):
        return remote(
            o_send.at[s, slot],
            o_recv.at[s, slot],
            o_ss.at[s, slot],
            o_rs.at[s, slot],
            z_peer((nz - AWAY[slot]) % nz),
        )

    def zs_copy(slot):
        return remote(
            zs_send.at[slot],
            zs_recv.at[slot],
            s_ss.at[slot],
            s_rs.at[slot],
            z_peer((nz - AWAY[slot]) % nz),
        )

    block = min(512, span)
    blocks = span // block

    def attend(s):
        for e in range(2):
            rows = q_buf[s, :, :, e * heads : (e + 1) * heads, :].astype(F32)
            qfull[:, e * half : (e + 1) * half] = rows.reshape(every, half).astype(BF16)
        ropes = r_buf[...].astype(F32).reshape(nctx, 2, heads, 2 * rope)
        odd = lax.rem(s, 2) == 1
        ropes = jnp.where(odd, ropes[:, 1], ropes[:, 0]).reshape(every, 2 * rope)
        late = s >= seqs // 2
        qfull[:, lat:] = jnp.where(late, ropes[:, rope:], ropes[:, :rope]).astype(BF16)
        top = jnp.full((every, 128), -1e30, F32)
        live = lengths[s] - c * span
        for b in range(blocks):
            part = jnp.dot(
                qfull[...],
                cache[s, :, b * block : (b + 1) * block],
                preferred_element_type=F32,
            )
            position = b * block + lax.broadcasted_iota(jnp.int32, part.shape, 1)
            part = jnp.where(position < live, part, -1e30)
            scores[:, b * block : (b + 1) * block] = part
            for e in range(block // 128):
                top = jnp.maximum(top, part[:, e * 128 : (e + 1) * 128])
        m2 = jnp.maximum(jnp.max(top, axis=1, keepdims=True) * scale2, FLOOR)
        total = jnp.zeros((every, 128), F32)
        for b in range(blocks):
            part = jnp.exp2(scores[:, b * block : (b + 1) * block] * scale2 - m2)
            probs[:, b * block : (b + 1) * block] = part.astype(BF16)
            for e in range(block // 128):
                total = total + part[:, e * 128 : (e + 1) * 128]
        l = jnp.sum(total, axis=1, keepdims=True)
        table = columns((every, 128), ((0, m2), (1, l)))
        st_mine[s, 0] = table[: every // 2]
        st_mine[s, 1] = table[every // 2 :]
        st_copy(s).start()
        acc = jnp.dot(probs[...], values[s], preferred_element_type=F32).astype(BF16)
        acc_mine[s, 0] = acc[: every // 2]
        acc_mine[s, 1] = acc[every // 2 :]
        acc_copy(s).start()

    def combine(s, last):
        st_copy(s).wait_recv()
        mine, theirs = st_mine[s, k], st_other[s]
        m_a, l_a = mine[:, 0:1], mine[:, 1:2]
        m_b, l_b = theirs[:, 0:1], theirs[:, 1:2]
        m = jnp.maximum(m_a, m_b)
        w_a, w_b = jnp.exp2(m_a - m), jnp.exp2(m_b - m)
        l = w_a * l_a + w_b * l_b
        table = columns((nz * heads, 128), ((2 * s, m), (2 * s + 1, l))).reshape(nz, heads, 128)
        if last:
            zs_send[...] += table

            for slot in range(nz - 1, 0, -1):
                zs_copy(slot).start()
            zs_recv[0] = zs_send[0]
        else:
            zs_send[...] += table
        acc_copy(s).wait_recv()
        joined = w_a * acc_mine[s, k].astype(F32) + w_b * acc_other[s].astype(F32)
        joined = joined.reshape(nz, heads, lat)
        joined = jnp.concatenate([joined[:, :, :half], joined[:, :, half:]], axis=1)
        o_send[s] = joined.astype(BF16)

        for slot in range(nz - 1, 0, -1):
            o_copy(s, slot).start()
        o_recv[s, 0] = o_send[s, 0]

    zs_send[...] = jnp.zeros_like(zs_send)
    pass_over(seqs)
    pass_over(0)
    hand(seqs, other).wait_recv()
    loads[3].wait()

    def step(s):
        @pl.when(s + 1 < seqs)
        def _():
            pass_over(s + 1)

        hand(s, other).wait_recv()
        attend(s)

        @pl.when(s > 0)
        def _():
            combine(s - 1, False)

    loop(seqs, step)
    combine(seqs - 1, True)

    def h_copy(p, d, slot):
        ref = heads_buf.at[p, slot]
        return remote(ref, ref, h_ss.at[p, d], h_rs.at[p, d], (dp_at(d), c))

    loads[4].wait()

    for slot in range(1, nz):
        zs_copy(slot).wait_recv()

    def finish(s, row):
        for slot in range(1, nz):
            o_copy(s, slot).wait_recv()
        lane = lax.broadcasted_iota(jnp.int32, (nz, heads, 128), 2)
        table = zs_recv[...]
        m = jnp.sum(jnp.where(lane == 2 * s, table, 0.0), axis=2, keepdims=True)
        l = jnp.sum(jnp.where(lane == 2 * s + 1, table, 0.0), axis=2, keepdims=True)
        top = jnp.max(m, axis=0, keepdims=True)
        w = jnp.exp2(m - top)
        w = w / jnp.sum(w * l, axis=0, keepdims=True)
        data = o_recv[s].astype(F32)
        left = jnp.sum(w * data[:, :heads], axis=0)
        right = jnp.sum(w * data[:, heads:], axis=0)
        latents[pl.ds(row, heads), :] = jnp.concatenate([left, right], axis=1)

    def project(p):
        for e in range(seqs // 2):
            finish(p * (seqs // 2) + e, e * heads)
        head_out = jnp.dot(
            spread(latents[...].astype(BF16), heads), wuv[...], preferred_element_type=F32
        )
        heads_buf[p, i] = head_out.astype(BF16)

        for d in far_first(ndp):
            h_copy(p, d, i).start()

    loop(2, project)

    for p in range(2):
        for d in near_first(ndp):
            h_copy(p, d, dp_at(ndp - d)).wait_recv()
    heads_f32[...] = heads_buf[...].astype(F32).reshape(heads_f32.shape)
    rows = ndp * seqs
    merged = jnp.concatenate(
        [heads_f32[pl.ds(h, rows, stride=heads), :] for h in range(heads)], axis=1
    ).astype(BF16)
    terms = jnp.dot(merged, wout_t[...], preferred_element_type=F32)
    cols = terms.shape[1]
    pieces = -(-cols // 128)
    for p in range(2):
        for n in range(pieces):
            piece = terms[p * rows // 2 : (p + 1) * rows // 2, n * 128 : min(cols, (n + 1) * 128)]
            if piece.shape[1] < 128:
                piece = jnp.concatenate(
                    [piece, jnp.zeros((rows // 2, 128 - piece.shape[1]), F32)], axis=1
                )
            sums_f32[pl.ds(p * pieces + n, rows // 2, stride=2 * pieces), :] = piece
    sums_send[...] = sums_f32[...].astype(BF16).reshape(sums_send.shape)

    def t_copy(d, at, slot):
        return remote(
            sums_send.at[at], sums_recv.at[slot], t_ss.at[d], t_rs.at[d], (i, ctx_at(d))
        )

    for d in far_first(nctx):
        t_copy(d, ctx_at(d), c).start()
    sums_recv[c] = sums_send[c]

    for slot in range(1, nz):
        zs_copy(slot).wait_send()
        give(seqs, slot).wait_send()
    hand(seqs, k).wait_send()

    def sent(s):
        hand(s, k).wait_send()
        for slot in range(1, nz):
            give(s, slot).wait_send()
        st_copy(s).wait_send()
        acc_copy(s).wait_send()
        for slot in range(1, nz):
            o_copy(s, slot).wait_send()

    loop(seqs, sent)

    def sent_heads(n):
        h_copy(0, n + 1, i).wait_send()
        h_copy(1, n + 1, i).wait_send()

    loop(ndp - 1, sent_heads)

    for d in far_first(nctx):
        t_copy(d, ctx_at(d), c).wait_send()
    for d in near_first(nctx):
        came = ctx_at(nctx - d)
        t_copy(d, came, came).wait_recv()
    out_f32[...] = jnp.sum(sums_recv[...].astype(F32), axis=0)
    for p in range(2):
        for n in range(pieces):
            end = min(cols, (n + 1) * 128)
            piece = out_f32[pl.ds(p * pieces + n, seqs // 2, stride=2 * pieces), :]
            out_ref[p * seqs // 2 : (p + 1) * seqs // 2, n * 128 : end] = piece[
                :, : end - n * 128
            ].astype(BF16)


def per_device(nz, ndp, q_nope, q_rope, w_uk, w_uv, w_out, latent_cache, lengths):
    seqs, heads, dn = q_nope.shape
    rope = q_rope.shape[2]
    lat = w_uk.shape[2]
    span = latent_cache.shape[1]
    dv = w_uv.shape[2]
    cols = w_out.shape[1]
    nctx = 2 * nz
    every = nctx * heads
    own = nz * heads
    pieces = -(-cols // 128)
    scale2 = math.log2(math.e) / math.sqrt(dn + rope)
    vmem, dma = pltpu.VMEM, pltpu.SemaphoreType.DMA
    hbm = pl.BlockSpec(memory_space=pltpu.HBM)
    return pl.pallas_call(
        functools.partial(kernel, nz, ndp, scale2),
        out_shape=jax.ShapeDtypeStruct((seqs, cols), BF16),
        in_specs=[hbm] * 7,
        out_specs=pl.BlockSpec(memory_space=vmem),
        scratch_shapes=[
            pltpu.SMEM((seqs,), jnp.int32),
            vmem((seqs * heads, dn), BF16),
            vmem((seqs * heads, rope), BF16),
            vmem((heads * dn, lat), BF16),
            vmem((heads * lat, dv), BF16),
            vmem((cols, heads * dv), BF16),
            vmem((heads * dv, cols), BF16),
            vmem((seqs, lat + rope, span), BF16),
            vmem((seqs, span, lat), BF16),
            vmem((seqs, 2, nz, 2 * heads, lat // 2), BF16),
            vmem((2, nz, 2 * heads, 2 * rope), BF16),
            vmem((every, lat + rope), BF16),
            vmem((every, span), F32),
            vmem((every, span), BF16),
            vmem((seqs, 2, own, 128), F32),
            vmem((seqs, own, 128), F32),
            vmem((seqs, 2, own, lat), BF16),
            vmem((seqs, own, lat), BF16),
            vmem((nz, heads, 128), F32),
            vmem((nz, heads, 128), F32),
            vmem((seqs, nz, 2 * heads, lat // 2), BF16),
            vmem((seqs, nz, 2 * heads, lat // 2), BF16),
            vmem((seqs // 2 * heads, lat), F32),
            vmem((2, ndp, seqs // 2 * heads, dv), BF16),
            vmem((ndp * seqs * heads, dv), F32),
            vmem((ndp * seqs * pieces, 128), F32),
            vmem((nctx, seqs * pieces, 128), BF16),
            vmem((nctx, seqs * pieces, 128), BF16),
            vmem((seqs * pieces, 128), F32),
            dma((6,)),
            dma((seqs,)),
            dma((seqs + 1, nz)),
            dma((seqs + 1, nz)),
            dma((seqs + 1,)),
            dma((seqs + 1,)),
            dma((seqs, 2)),
            dma((seqs, 2)),
            dma((nz,)),
            dma((nz,)),
            dma((seqs, nz)),
            dma((seqs, nz)),
            dma((2, ndp)),
            dma((2, ndp)),
            dma((nctx,)),
            dma((nctx,)),
        ],
        compiler_params=pltpu.CompilerParams(
            collective_id=0, has_side_effects=True, vmem_limit_bytes=60 << 20
        ),
        name="mla_decode",
    )(
        lengths,
        q_nope.reshape(seqs * heads, dn),
        q_rope.reshape(seqs * heads, rope),
        w_uk.reshape(heads * dn, lat),
        w_uv.reshape(heads * lat, dv),
        w_out.T,
        jnp.swapaxes(latent_cache, 1, 2),
    )


def solution(mesh):
    in_specs = (
        P("dp", "ctx", None),
        P("dp", "ctx", None),
        P("ctx", None, None),
        P("ctx", None, None),
        P("ctx", "dp"),
        P("dp", "ctx", None),
        P("dp"),
    )
    out_specs = P("ctx", "dp")
    return jax.shard_map(
        functools.partial(per_device, mesh.shape["ctx"] // 2, mesh.shape["dp"]),
        mesh=mesh,
        in_specs=in_specs,
        out_specs=out_specs,
        check_vma=False,
    )
```

```python
import functools
import math

import jax
import jax.numpy as jnp
from jax import lax
from jax.experimental import pallas as pl
from jax.experimental.pallas import tpu as pltpu
from jax.sharding import PartitionSpec as P

MESH = pl.DeviceIdType.MESH
F32 = jnp.float32
BF16 = jnp.bfloat16
FLOOR = -(2.0**90)


def far_first(size):
    return sorted(range(1, size), key=lambda d: -min(d, size - d))


def near_first(size):
    return sorted(range(1, size), key=lambda d: min(d, size - d))


AWAY = (0, 1, 7, 2, 6, 3, 5, 4)


def loop(count, body):
    lax.fori_loop(0, count, lambda n, carry: (body(n), carry)[1], 0)


def columns(shape, values):
    lane = lax.broadcasted_iota(jnp.int32, shape, 1)
    out = jnp.zeros(shape, F32)
    for at, value in values:
        out = jnp.where(lane == at, value, out)
    return out


def spread(rows, heads):
    count, width = rows.shape
    wide = jnp.concatenate([rows.astype(F32)] * heads, axis=1)
    row_head = lax.rem(lax.broadcasted_iota(jnp.int32, wide.shape, 0), heads)
    col_head = lax.div(lax.broadcasted_iota(jnp.int32, wide.shape, 1), width)
    return jnp.where(row_head == col_head, wide, 0.0).astype(BF16)


def remote(src, dst, ss, rs, device):
    return pltpu.make_async_remote_copy(
        src_ref=src, dst_ref=dst, send_sem=ss, recv_sem=rs, device_id=device, device_id_type=MESH
    )


def kernel(
    nz,
    ndp,
    scale2,
    len_hbm,
    qn_hbm,
    qr_hbm,
    wuk_hbm,
    wuv_hbm,
    wout_hbm,
    cache_hbm,
    out_ref,
    lengths,
    qn,
    qr,
    wuk,
    wuv,
    wout,
    wout_t,
    cache,
    values,
    q_buf,
    r_buf,
    qfull,
    scores,
    probs,
    st_mine,
    st_other,
    acc_mine,
    acc_other,
    zs_send,
    zs_recv,
    o_send,
    o_recv,
    latents,
    heads_buf,
    heads_f32,
    sums_f32,
    sums_send,
    sums_recv,
    out_f32,
    load_sem,
    cache_sem,
    q_ss,
    q_rs,
    f_ss,
    f_rs,
    p_ss,
    p_rs,
    s_ss,
    s_rs,
    o_ss,
    o_rs,
    h_ss,
    h_rs,
    t_ss,
    t_rs,
):
    nctx = 2 * nz
    i = lax.axis_index("dp")
    c = lax.axis_index("ctx")
    z = lax.div(c, 2)
    k = lax.rem(c, 2)
    other = 1 - k
    seqs, width, span = cache.shape
    lat = wuk.shape[1]
    rope = width - lat
    heads = wuk.shape[0] // qn.shape[1]
    every = nctx * heads
    half = lat // 2

    def z_at(d):
        return lax.rem(z + d, nz)

    def z_peer(d):
        return (i, z_at(d) * 2 + k)

    partner = (i, z * 2 + other)

    def ctx_at(d):
        return lax.rem(c + d, nctx)

    def dp_at(d):
        return lax.rem(i + d, ndp)

    loads = [
        pltpu.make_async_copy(src, dst, load_sem.at[n])
        for n, (src, dst) in enumerate(
            (
                (wuk_hbm, wuk),
                (qn_hbm, qn),
                (qr_hbm, qr),
                (len_hbm, lengths),
                (wuv_hbm, wuv),
                (wout_hbm, wout),
            )
        )
    ]

    def cache_load(s):
        return pltpu.make_async_copy(cache_hbm.at[s], cache.at[s], cache_sem.at[s])

    loads[0].start()
    loads[1].start()

    barrier = pltpu.get_barrier_semaphore()

    def greet(peer):
        pl.semaphore_signal(barrier, inc=1, device_id=peer, device_id_type=MESH)

    for slot in range(nz - 1, 0, -1):
        greet(z_peer(AWAY[slot]))
    greet(partner)
    for d in range(1, ndp):
        greet((dp_at(d), c))

    loads[2].start()
    loads[3].start()
    loop(seqs, lambda s: cache_load(s).start())
    loads[4].start()
    loads[5].start()

    loads[2].wait()
    rows = qr[...].astype(F32)
    mid = seqs * heads // 2
    r_buf[k, 0] = jnp.concatenate([rows[:mid], rows[mid:]], axis=1).astype(BF16)

    loads[0].wait()
    loads[1].wait()
    q_lat = jnp.dot(spread(qn[...], heads), wuk[...], preferred_element_type=F32)
    for s in range(seqs):
        rows = q_lat[s * heads : (s + 1) * heads]
        q_buf[s, k, 0] = jnp.concatenate([rows[:, :half], rows[:, half:]], axis=0).astype(BF16)

    pl.semaphore_wait(barrier, nz + ndp - 1)

    def block_of(s, core, slot):
        return r_buf.at[core, slot] if isinstance(s, int) and s == seqs else q_buf.at[s, core, slot]

    def give(s, slot):
        return remote(
            block_of(s, k, 0),
            block_of(s, k, slot),
            q_ss.at[s, slot],
            q_rs.at[s, slot],
            z_peer(AWAY[slot]),
        )

    def hand(s, core):
        ref = r_buf.at[core] if isinstance(s, int) and s == seqs else q_buf.at[s, core]
        return remote(ref, ref, f_ss.at[s], f_rs.at[s], partner)

    order = (seqs,) + tuple(range(seqs))
    for s in order:
        for slot in range(nz - 1, 0, -1):
            give(s, slot).start()

    def pass_over(s):
        for slot in range(1, nz):
            give(s, slot).wait_recv()
        hand(s, k).start()

    def turn(s):
        cache_load(s).wait()
        for b in range(span // 256):
            part = cache[s, :lat, b * 256 : (b + 1) * 256]
            values[s, b * 256 : (b + 1) * 256, :] = part.T

    loop(seqs, turn)
    loads[5].wait()
    wout_t[...] = wout[...].T

    def st_copy(s):
        return remote(
            st_mine.at[s, other], st_other.at[s], p_ss.at[s, 0], p_rs.at[s, 0], partner
        )

    def acc_copy(s):
        return remote(
            acc_mine.at[s, other], acc_other.at[s], p_ss.at[s, 1], p_rs.at[s, 1], partner
        )

    def o_copy(s, slot):
        return remote(
            o_send.at[s, slot],
            o_recv.at[s, slot],
            o_ss.at[s, slot],
            o_rs.at[s, slot],
            z_peer((nz - AWAY[slot]) % nz),
        )

    def zs_copy(slot):
        return remote(
            zs_send.at[slot],
            zs_recv.at[slot],
            s_ss.at[slot],
            s_rs.at[slot],
            z_peer((nz - AWAY[slot]) % nz),
        )

    block = min(512, span)
    blocks = span // block

    def attend(s):
        for e in range(2):
            rows = q_buf[s, :, :, e * heads : (e + 1) * heads, :].astype(F32)
            qfull[:, e * half : (e + 1) * half] = rows.reshape(every, half).astype(BF16)
        ropes = r_buf[...].astype(F32).reshape(nctx, 2, heads, 2 * rope)
        odd = lax.rem(s, 2) == 1
        ropes = jnp.where(odd, ropes[:, 1], ropes[:, 0]).reshape(every, 2 * rope)
        late = s >= seqs // 2
        qfull[:, lat:] = jnp.where(late, ropes[:, rope:], ropes[:, :rope]).astype(BF16)
        top = jnp.full((every, 128), -1e30, F32)
        live = lengths[s] - c * span
        for b in range(blocks):
            part = jnp.dot(
                qfull[...],
                cache[s, :, b * block : (b + 1) * block],
                preferred_element_type=F32,
            )
            position = b * block + lax.broadcasted_iota(jnp.int32, part.shape, 1)
            part = jnp.where(position < live, part, -1e30)
            scores[:, b * block : (b + 1) * block] = part
            for e in range(block // 128):
                top = jnp.maximum(top, part[:, e * 128 : (e + 1) * 128])
        m2 = jnp.maximum(jnp.max(top, axis=1, keepdims=True) * scale2, FLOOR)
        total = jnp.zeros((every, 128), F32)
        for b in range(blocks):
            part = jnp.exp2(scores[:, b * block : (b + 1) * block] * scale2 - m2)
            probs[:, b * block : (b + 1) * block] = part.astype(BF16)
            for e in range(block // 128):
                total = total + part[:, e * 128 : (e + 1) * 128]
        l = jnp.sum(total, axis=1, keepdims=True)
        table = columns((every, 128), ((0, m2), (1, l)))
        st_mine[s, 0] = table[: every // 2]
        st_mine[s, 1] = table[every // 2 :]
        st_copy(s).start()
        acc = jnp.dot(probs[...], values[s], preferred_element_type=F32).astype(BF16)
        acc_mine[s, 0] = acc[: every // 2]
        acc_mine[s, 1] = acc[every // 2 :]
        acc_copy(s).start()

    def combine(s, last):
        st_copy(s).wait_recv()
        mine, theirs = st_mine[s, k], st_other[s]
        m_a, l_a = mine[:, 0:1], mine[:, 1:2]
        m_b, l_b = theirs[:, 0:1], theirs[:, 1:2]
        m = jnp.maximum(m_a, m_b)
        w_a, w_b = jnp.exp2(m_a - m), jnp.exp2(m_b - m)
        l = w_a * l_a + w_b * l_b
        table = columns((nz * heads, 128), ((2 * s, m), (2 * s + 1, l))).reshape(nz, heads, 128)
        if last:
            zs_send[...] += table

            for slot in range(nz - 1, 0, -1):
                zs_copy(slot).start()
            zs_recv[0] = zs_send[0]
        else:
            zs_send[...] += table
        acc_copy(s).wait_recv()
        joined = w_a * acc_mine[s, k].astype(F32) + w_b * acc_other[s].astype(F32)
        joined = joined.reshape(nz, heads, lat)
        joined = jnp.concatenate([joined[:, :, :half], joined[:, :, half:]], axis=1)
        o_send[s] = joined.astype(BF16)

        for slot in range(nz - 1, 0, -1):
            o_copy(s, slot).start()
        o_recv[s, 0] = o_send[s, 0]

    zs_send[...] = jnp.zeros_like(zs_send)
    pass_over(seqs)
    pass_over(0)
    hand(seqs, other).wait_recv()
    loads[3].wait()

    def step(s):
        @pl.when(s + 1 < seqs)
        def _():
            pass_over(s + 1)

        hand(s, other).wait_recv()
        attend(s)

        @pl.when(s > 0)
        def _():
            combine(s - 1, False)

    for s in range(seqs):
        step(s)
    combine(seqs - 1, True)

    def h_copy(p, d, slot):
        ref = heads_buf.at[p, slot]
        return remote(ref, ref, h_ss.at[p, d], h_rs.at[p, d], (dp_at(d), c))

    loads[4].wait()

    for slot in range(1, nz):
        zs_copy(slot).wait_recv()

    def finish(s, row):
        for slot in range(1, nz):
            o_copy(s, slot).wait_recv()
        lane = lax.broadcasted_iota(jnp.int32, (nz, heads, 128), 2)
        table = zs_recv[...]
        m = jnp.sum(jnp.where(lane == 2 * s, table, 0.0), axis=2, keepdims=True)
        l = jnp.sum(jnp.where(lane == 2 * s + 1, table, 0.0), axis=2, keepdims=True)
        top = jnp.max(m, axis=0, keepdims=True)
        w = jnp.exp2(m - top)
        w = w / jnp.sum(w * l, axis=0, keepdims=True)
        data = o_recv[s].astype(F32)
        left = jnp.sum(w * data[:, :heads], axis=0)
        right = jnp.sum(w * data[:, heads:], axis=0)
        latents[pl.ds(row, heads), :] = jnp.concatenate([left, right], axis=1)

    def project(p):
        for e in range(seqs // 2):
            finish(p * (seqs // 2) + e, e * heads)
        head_out = jnp.dot(
            spread(latents[...].astype(BF16), heads), wuv[...], preferred_element_type=F32
        )
        heads_buf[p, i] = head_out.astype(BF16)

        for d in far_first(ndp):
            h_copy(p, d, i).start()

    for p in range(2):
        project(p)

    for p in range(2):
        for d in near_first(ndp):
            h_copy(p, d, dp_at(ndp - d)).wait_recv()
    heads_f32[...] = heads_buf[...].astype(F32).reshape(heads_f32.shape)
    rows = ndp * seqs
    merged = jnp.concatenate(
        [heads_f32[pl.ds(h, rows, stride=heads), :] for h in range(heads)], axis=1
    ).astype(BF16)
    terms = jnp.dot(merged, wout_t[...], preferred_element_type=F32)
    cols = terms.shape[1]
    pieces = -(-cols // 128)
    for p in range(2):
        for n in range(pieces):
            piece = terms[p * rows // 2 : (p + 1) * rows // 2, n * 128 : min(cols, (n + 1) * 128)]
            if piece.shape[1] < 128:
                piece = jnp.concatenate(
                    [piece, jnp.zeros((rows // 2, 128 - piece.shape[1]), F32)], axis=1
                )
            sums_f32[pl.ds(p * pieces + n, rows // 2, stride=2 * pieces), :] = piece
    sums_send[...] = sums_f32[...].astype(BF16).reshape(sums_send.shape)

    def t_copy(d, at, slot):
        return remote(
            sums_send.at[at], sums_recv.at[slot], t_ss.at[d], t_rs.at[d], (i, ctx_at(d))
        )

    for d in far_first(nctx):
        t_copy(d, ctx_at(d), c).start()
    sums_recv[c] = sums_send[c]

    for slot in range(1, nz):
        zs_copy(slot).wait_send()
        give(seqs, slot).wait_send()
    hand(seqs, k).wait_send()

    def sent(s):
        hand(s, k).wait_send()
        for slot in range(1, nz):
            give(s, slot).wait_send()
        st_copy(s).wait_send()
        acc_copy(s).wait_send()
        for slot in range(1, nz):
            o_copy(s, slot).wait_send()

    loop(seqs, sent)

    def sent_heads(n):
        h_copy(0, n + 1, i).wait_send()
        h_copy(1, n + 1, i).wait_send()

    loop(ndp - 1, sent_heads)

    for d in far_first(nctx):
        t_copy(d, ctx_at(d), c).wait_send()
    for d in near_first(nctx):
        came = ctx_at(nctx - d)
        t_copy(d, came, came).wait_recv()
    out_f32[...] = jnp.sum(sums_recv[...].astype(F32), axis=0)
    for p in range(2):
        for n in range(pieces):
            end = min(cols, (n + 1) * 128)
            piece = out_f32[pl.ds(p * pieces + n, seqs // 2, stride=2 * pieces), :]
            out_ref[p * seqs // 2 : (p + 1) * seqs // 2, n * 128 : end] = piece[
                :, : end - n * 128
            ].astype(BF16)


def per_device(nz, ndp, q_nope, q_rope, w_uk, w_uv, w_out, latent_cache, lengths):
    seqs, heads, dn = q_nope.shape
    rope = q_rope.shape[2]
    lat = w_uk.shape[2]
    span = latent_cache.shape[1]
    dv = w_uv.shape[2]
    cols = w_out.shape[1]
    nctx = 2 * nz
    every = nctx * heads
    own = nz * heads
    pieces = -(-cols // 128)
    scale2 = math.log2(math.e) / math.sqrt(dn + rope)
    vmem, dma = pltpu.VMEM, pltpu.SemaphoreType.DMA
    hbm = pl.BlockSpec(memory_space=pltpu.HBM)
    return pl.pallas_call(
        functools.partial(kernel, nz, ndp, scale2),
        out_shape=jax.ShapeDtypeStruct((seqs, cols), BF16),
        in_specs=[hbm] * 7,
        out_specs=pl.BlockSpec(memory_space=vmem),
        scratch_shapes=[
            pltpu.SMEM((seqs,), jnp.int32),
            vmem((seqs * heads, dn), BF16),
            vmem((seqs * heads, rope), BF16),
            vmem((heads * dn, lat), BF16),
            vmem((heads * lat, dv), BF16),
            vmem((cols, heads * dv), BF16),
            vmem((heads * dv, cols), BF16),
            vmem((seqs, lat + rope, span), BF16),
            vmem((seqs, span, lat), BF16),
            vmem((seqs, 2, nz, 2 * heads, lat // 2), BF16),
            vmem((2, nz, 2 * heads, 2 * rope), BF16),
            vmem((every, lat + rope), BF16),
            vmem((every, span), F32),
            vmem((every, span), BF16),
            vmem((seqs, 2, own, 128), F32),
            vmem((seqs, own, 128), F32),
            vmem((seqs, 2, own, lat), BF16),
            vmem((seqs, own, lat), BF16),
            vmem((nz, heads, 128), F32),
            vmem((nz, heads, 128), F32),
            vmem((seqs, nz, 2 * heads, lat // 2), BF16),
            vmem((seqs, nz, 2 * heads, lat // 2), BF16),
            vmem((seqs // 2 * heads, lat), F32),
            vmem((2, ndp, seqs // 2 * heads, dv), BF16),
            vmem((ndp * seqs * heads, dv), F32),
            vmem((ndp * seqs * pieces, 128), F32),
            vmem((nctx, seqs * pieces, 128), BF16),
            vmem((nctx, seqs * pieces, 128), BF16),
            vmem((seqs * pieces, 128), F32),
            dma((6,)),
            dma((seqs,)),
            dma((seqs + 1, nz)),
            dma((seqs + 1, nz)),
            dma((seqs + 1,)),
            dma((seqs + 1,)),
            dma((seqs, 2)),
            dma((seqs, 2)),
            dma((nz,)),
            dma((nz,)),
            dma((seqs, nz)),
            dma((seqs, nz)),
            dma((2, ndp)),
            dma((2, ndp)),
            dma((nctx,)),
            dma((nctx,)),
        ],
        compiler_params=pltpu.CompilerParams(
            collective_id=0, has_side_effects=True, vmem_limit_bytes=60 << 20
        ),
        name="mla_decode",
    )(
        lengths,
        q_nope.reshape(seqs * heads, dn),
        q_rope.reshape(seqs * heads, rope),
        w_uk.reshape(heads * dn, lat),
        w_uv.reshape(heads * lat, dv),
        w_out.T,
        jnp.swapaxes(latent_cache, 1, 2),
    )


def solution(mesh):
    in_specs = (
        P("dp", "ctx", None),
        P("dp", "ctx", None),
        P("ctx", None, None),
        P("ctx", None, None),
        P("ctx", "dp"),
        P("dp", "ctx", None),
        P("dp"),
    )
    out_specs = P("ctx", "dp")
    return jax.shard_map(
        functools.partial(per_device, mesh.shape["ctx"] // 2, mesh.shape["dp"]),
        mesh=mesh,
        in_specs=in_specs,
        out_specs=out_specs,
        check_vma=False,
    )
```

```python
import functools
import math

import jax
import jax.numpy as jnp
from jax import lax
from jax.experimental import pallas as pl
from jax.experimental.pallas import tpu as pltpu
from jax.sharding import PartitionSpec as P

MESH = pl.DeviceIdType.MESH
F32 = jnp.float32
BF16 = jnp.bfloat16
FLOOR = -(2.0**90)


def far_first(size):
    return sorted(range(1, size), key=lambda d: -min(d, size - d))


def near_first(size):
    return sorted(range(1, size), key=lambda d: min(d, size - d))


AWAY = (0, 1, 7, 2, 6, 3, 5, 4)


def loop(count, body):
    lax.fori_loop(0, count, lambda n, carry: (body(n), carry)[1], 0)


def columns(shape, values):
    lane = lax.broadcasted_iota(jnp.int32, shape, 1)
    out = jnp.zeros(shape, F32)
    for at, value in values:
        out = jnp.where(lane == at, value, out)
    return out


def spread(rows, heads):
    count, width = rows.shape
    wide = jnp.concatenate([rows.astype(F32)] * heads, axis=1)
    row_head = lax.rem(lax.broadcasted_iota(jnp.int32, wide.shape, 0), heads)
    col_head = lax.div(lax.broadcasted_iota(jnp.int32, wide.shape, 1), width)
    return jnp.where(row_head == col_head, wide, 0.0).astype(BF16)


def remote(src, dst, ss, rs, device):
    return pltpu.make_async_remote_copy(
        src_ref=src, dst_ref=dst, send_sem=ss, recv_sem=rs, device_id=device, device_id_type=MESH
    )


def kernel(
    nz,
    ndp,
    scale2,
    len_hbm,
    qn_hbm,
    qr_hbm,
    wuk_hbm,
    wuv_hbm,
    wout_hbm,
    cache_hbm,
    out_ref,
    lengths,
    qn,
    qr,
    wuk,
    wuv,
    wout,
    wout_t,
    cache,
    values,
    q_buf,
    r_buf,
    qfull,
    scores,
    probs,
    st_mine,
    st_other,
    acc_mine,
    acc_other,
    zs_send,
    zs_recv,
    o_send,
    o_recv,
    latents,
    heads_buf,
    heads_f32,
    sums_f32,
    sums_send,
    sums_recv,
    out_f32,
    load_sem,
    cache_sem,
    q_ss,
    q_rs,
    f_ss,
    f_rs,
    p_ss,
    p_rs,
    s_ss,
    s_rs,
    o_ss,
    o_rs,
    h_ss,
    h_rs,
    t_ss,
    t_rs,
):
    nctx = 2 * nz
    i = lax.axis_index("dp")
    c = lax.axis_index("ctx")
    z = lax.div(c, 2)
    k = lax.rem(c, 2)
    other = 1 - k
    seqs, width, span = cache.shape
    lat = wuk.shape[1]
    rope = width - lat
    heads = wuk.shape[0] // qn.shape[1]
    every = nctx * heads
    half = lat // 2

    def z_at(d):
        return lax.rem(z + d, nz)

    def z_peer(d):
        return (i, z_at(d) * 2 + k)

    partner = (i, z * 2 + other)

    def ctx_at(d):
        return lax.rem(c + d, nctx)

    def dp_at(d):
        return lax.rem(i + d, ndp)

    loads = [
        pltpu.make_async_copy(src, dst, load_sem.at[n])
        for n, (src, dst) in enumerate(
            (
                (wuk_hbm, wuk),
                (qn_hbm, qn),
                (qr_hbm, qr),
                (len_hbm, lengths),
                (wuv_hbm, wuv),
                (wout_hbm, wout),
            )
        )
    ]

    def cache_load(s):
        return pltpu.make_async_copy(cache_hbm.at[s], cache.at[s], cache_sem.at[s])

    loads[0].start()
    loads[1].start()

    barrier = pltpu.get_barrier_semaphore()

    def greet(peer):
        pl.semaphore_signal(barrier, inc=1, device_id=peer, device_id_type=MESH)

    for slot in range(nz - 1, 0, -1):
        greet(z_peer(AWAY[slot]))
    greet(partner)
    for d in range(1, ndp):
        greet((dp_at(d), c))

    loads[2].start()
    loads[3].start()
    loop(seqs, lambda s: cache_load(s).start())
    loads[4].start()
    loads[5].start()

    loads[2].wait()
    rows = qr[...].astype(F32)
    mid = seqs * heads // 2
    r_buf[k, 0] = jnp.concatenate([rows[:mid], rows[mid:]], axis=1).astype(BF16)

    loads[0].wait()
    loads[1].wait()
    q_lat = jnp.dot(spread(qn[...], heads), wuk[...], preferred_element_type=F32)
    for s in range(seqs):
        rows = q_lat[s * heads : (s + 1) * heads]
        q_buf[s, k, 0] = jnp.concatenate([rows[:, :half], rows[:, half:]], axis=0).astype(BF16)

    pl.semaphore_wait(barrier, nz + ndp - 1)

    def block_of(s, core, slot):
        return r_buf.at[core, slot] if isinstance(s, int) and s == seqs else q_buf.at[s, core, slot]

    def give(s, slot):
        return remote(
            block_of(s, k, 0),
            block_of(s, k, slot),
            q_ss.at[s, slot],
            q_rs.at[s, slot],
            z_peer(AWAY[slot]),
        )

    def hand(s, core):
        ref = r_buf.at[core] if isinstance(s, int) and s == seqs else q_buf.at[s, core]
        return remote(ref, ref, f_ss.at[s], f_rs.at[s], partner)

    order = (seqs,) + tuple(range(seqs))
    for s in order:
        for slot in range(nz - 1, 0, -1):
            give(s, slot).start()

    def pass_over(s):
        for slot in range(1, nz):
            give(s, slot).wait_recv()
        hand(s, k).start()

    def turn(s):
        cache_load(s).wait()
        for b in range(span // 256):
            part = cache[s, :lat, b * 256 : (b + 1) * 256]
            values[s, b * 256 : (b + 1) * 256, :] = part.T

    for s in range(seqs):
        turn(s)
    loads[5].wait()
    wout_t[...] = wout[...].T

    def st_copy(s):
        return remote(
            st_mine.at[s, other], st_other.at[s], p_ss.at[s, 0], p_rs.at[s, 0], partner
        )

    def acc_copy(s):
        return remote(
            acc_mine.at[s, other], acc_other.at[s], p_ss.at[s, 1], p_rs.at[s, 1], partner
        )

    def o_copy(s, slot):
        return remote(
            o_send.at[s, slot],
            o_recv.at[s, slot],
            o_ss.at[s, slot],
            o_rs.at[s, slot],
            z_peer((nz - AWAY[slot]) % nz),
        )

    def zs_copy(slot):
        return remote(
            zs_send.at[slot],
            zs_recv.at[slot],
            s_ss.at[slot],
            s_rs.at[slot],
            z_peer((nz - AWAY[slot]) % nz),
        )

    block = min(512, span)
    blocks = span // block

    def attend(s):
        for e in range(2):
            rows = q_buf[s, :, :, e * heads : (e + 1) * heads, :].astype(F32)
            qfull[:, e * half : (e + 1) * half] = rows.reshape(every, half).astype(BF16)
        ropes = r_buf[...].astype(F32).reshape(nctx, 2, heads, 2 * rope)
        odd = lax.rem(s, 2) == 1
        ropes = jnp.where(odd, ropes[:, 1], ropes[:, 0]).reshape(every, 2 * rope)
        late = s >= seqs // 2
        qfull[:, lat:] = jnp.where(late, ropes[:, rope:], ropes[:, :rope]).astype(BF16)
        top = jnp.full((every, 128), -1e30, F32)
        live = lengths[s] - c * span
        for b in range(blocks):
            part = jnp.dot(
                qfull[...],
                cache[s, :, b * block : (b + 1) * block],
                preferred_element_type=F32,
            )
            position = b * block + lax.broadcasted_iota(jnp.int32, part.shape, 1)
            part = jnp.where(position < live, part, -1e30)
            scores[:, b * block : (b + 1) * block] = part
            for e in range(block // 128):
                top = jnp.maximum(top, part[:, e * 128 : (e + 1) * 128])
        m2 = jnp.maximum(jnp.max(top, axis=1, keepdims=True) * scale2, FLOOR)
        total = jnp.zeros((every, 128), F32)
        for b in range(blocks):
            part = jnp.exp2(scores[:, b * block : (b + 1) * block] * scale2 - m2)
            probs[:, b * block : (b + 1) * block] = part.astype(BF16)
            for e in range(block // 128):
                total = total + part[:, e * 128 : (e + 1) * 128]
        l = jnp.sum(total, axis=1, keepdims=True)
        table = columns((every, 128), ((0, m2), (1, l)))
        st_mine[s, 0] = table[: every // 2]
        st_mine[s, 1] = table[every // 2 :]
        st_copy(s).start()
        acc = jnp.dot(probs[...], values[s], preferred_element_type=F32).astype(BF16)
        acc_mine[s, 0] = acc[: every // 2]
        acc_mine[s, 1] = acc[every // 2 :]
        acc_copy(s).start()

    def combine(s, last):
        st_copy(s).wait_recv()
        mine, theirs = st_mine[s, k], st_other[s]
        m_a, l_a = mine[:, 0:1], mine[:, 1:2]
        m_b, l_b = theirs[:, 0:1], theirs[:, 1:2]
        m = jnp.maximum(m_a, m_b)
        w_a, w_b = jnp.exp2(m_a - m), jnp.exp2(m_b - m)
        l = w_a * l_a + w_b * l_b
        table = columns((nz * heads, 128), ((2 * s, m), (2 * s + 1, l))).reshape(nz, heads, 128)
        if last:
            zs_send[...] += table

            for slot in range(nz - 1, 0, -1):
                zs_copy(slot).start()
            zs_recv[0] = zs_send[0]
        else:
            zs_send[...] += table
        acc_copy(s).wait_recv()
        joined = w_a * acc_mine[s, k].astype(F32) + w_b * acc_other[s].astype(F32)
        joined = joined.reshape(nz, heads, lat)
        joined = jnp.concatenate([joined[:, :, :half], joined[:, :, half:]], axis=1)
        o_send[s] = joined.astype(BF16)

        for slot in range(nz - 1, 0, -1):
            o_copy(s, slot).start()
        o_recv[s, 0] = o_send[s, 0]

    zs_send[...] = jnp.zeros_like(zs_send)
    pass_over(seqs)
    pass_over(0)
    hand(seqs, other).wait_recv()
    loads[3].wait()

    def step(s):
        @pl.when(s + 1 < seqs)
        def _():
            pass_over(s + 1)

        hand(s, other).wait_recv()
        attend(s)

        @pl.when(s > 0)
        def _():
            combine(s - 1, False)

    for s in range(seqs):
        step(s)
    combine(seqs - 1, True)

    def h_copy(p, d, slot):
        ref = heads_buf.at[p, slot]
        return remote(ref, ref, h_ss.at[p, d], h_rs.at[p, d], (dp_at(d), c))

    loads[4].wait()

    for slot in range(1, nz):
        zs_copy(slot).wait_recv()

    def finish(s, row):
        for slot in range(1, nz):
            o_copy(s, slot).wait_recv()
        lane = lax.broadcasted_iota(jnp.int32, (nz, heads, 128), 2)
        table = zs_recv[...]
        m = jnp.sum(jnp.where(lane == 2 * s, table, 0.0), axis=2, keepdims=True)
        l = jnp.sum(jnp.where(lane == 2 * s + 1, table, 0.0), axis=2, keepdims=True)
        top = jnp.max(m, axis=0, keepdims=True)
        w = jnp.exp2(m - top)
        w = w / jnp.sum(w * l, axis=0, keepdims=True)
        data = o_recv[s].astype(F32)
        left = jnp.sum(w * data[:, :heads], axis=0)
        right = jnp.sum(w * data[:, heads:], axis=0)
        latents[pl.ds(row, heads), :] = jnp.concatenate([left, right], axis=1)

    def project(p):
        for e in range(seqs // 2):
            finish(p * (seqs // 2) + e, e * heads)
        head_out = jnp.dot(
            spread(latents[...].astype(BF16), heads), wuv[...], preferred_element_type=F32
        )
        heads_buf[p, i] = head_out.astype(BF16)

        for d in far_first(ndp):
            h_copy(p, d, i).start()

    for p in range(2):
        project(p)

    rows = ndp * seqs // 2
    cols = wout_t.shape[1]
    pieces = -(-cols // 128)
    for p in range(2):
        for d in near_first(ndp):
            h_copy(p, d, dp_at(ndp - d)).wait_recv()
        heads_f32[p] = heads_buf[p].astype(F32).reshape(heads_f32.shape[1:])
        merged = jnp.concatenate(
            [heads_f32[p, pl.ds(h, rows, stride=heads), :] for h in range(heads)], axis=1
        ).astype(BF16)
        terms = jnp.dot(merged, wout_t[...], preferred_element_type=F32)
        for n in range(pieces):
            piece = terms[:, n * 128 : min(cols, (n + 1) * 128)]
            if piece.shape[1] < 128:
                piece = jnp.concatenate(
                    [piece, jnp.zeros((rows, 128 - piece.shape[1]), F32)], axis=1
                )
            sums_f32[pl.ds(p * pieces + n, rows, stride=2 * pieces), :] = piece
    sums_send[...] = sums_f32[...].astype(BF16).reshape(sums_send.shape)

    def t_copy(d, at, slot):
        return remote(
            sums_send.at[at], sums_recv.at[slot], t_ss.at[d], t_rs.at[d], (i, ctx_at(d))
        )

    for d in far_first(nctx):
        t_copy(d, ctx_at(d), c).start()
    sums_recv[c] = sums_send[c]

    for slot in range(1, nz):
        zs_copy(slot).wait_send()
        give(seqs, slot).wait_send()
    hand(seqs, k).wait_send()

    def sent(s):
        hand(s, k).wait_send()
        for slot in range(1, nz):
            give(s, slot).wait_send()
        st_copy(s).wait_send()
        acc_copy(s).wait_send()
        for slot in range(1, nz):
            o_copy(s, slot).wait_send()

    loop(seqs, sent)

    def sent_heads(n):
        h_copy(0, n + 1, i).wait_send()
        h_copy(1, n + 1, i).wait_send()

    loop(ndp - 1, sent_heads)

    for d in far_first(nctx):
        t_copy(d, ctx_at(d), c).wait_send()
    for d in near_first(nctx):
        came = ctx_at(nctx - d)
        t_copy(d, came, came).wait_recv()
    out_f32[...] = jnp.sum(sums_recv[...].astype(F32), axis=0)
    for p in range(2):
        for n in range(pieces):
            end = min(cols, (n + 1) * 128)
            piece = out_f32[pl.ds(p * pieces + n, seqs // 2, stride=2 * pieces), :]
            out_ref[p * seqs // 2 : (p + 1) * seqs // 2, n * 128 : end] = piece[
                :, : end - n * 128
            ].astype(BF16)


def per_device(nz, ndp, q_nope, q_rope, w_uk, w_uv, w_out, latent_cache, lengths):
    seqs, heads, dn = q_nope.shape
    rope = q_rope.shape[2]
    lat = w_uk.shape[2]
    span = latent_cache.shape[1]
    dv = w_uv.shape[2]
    cols = w_out.shape[1]
    nctx = 2 * nz
    every = nctx * heads
    own = nz * heads
    pieces = -(-cols // 128)
    scale2 = math.log2(math.e) / math.sqrt(dn + rope)
    vmem, dma = pltpu.VMEM, pltpu.SemaphoreType.DMA
    hbm = pl.BlockSpec(memory_space=pltpu.HBM)
    return pl.pallas_call(
        functools.partial(kernel, nz, ndp, scale2),
        out_shape=jax.ShapeDtypeStruct((seqs, cols), BF16),
        in_specs=[hbm] * 7,
        out_specs=pl.BlockSpec(memory_space=vmem),
        scratch_shapes=[
            pltpu.SMEM((seqs,), jnp.int32),
            vmem((seqs * heads, dn), BF16),
            vmem((seqs * heads, rope), BF16),
            vmem((heads * dn, lat), BF16),
            vmem((heads * lat, dv), BF16),
            vmem((cols, heads * dv), BF16),
            vmem((heads * dv, cols), BF16),
            vmem((seqs, lat + rope, span), BF16),
            vmem((seqs, span, lat), BF16),
            vmem((seqs, 2, nz, 2 * heads, lat // 2), BF16),
            vmem((2, nz, 2 * heads, 2 * rope), BF16),
            vmem((every, lat + rope), BF16),
            vmem((every, span), F32),
            vmem((every, span), BF16),
            vmem((seqs, 2, own, 128), F32),
            vmem((seqs, own, 128), F32),
            vmem((seqs, 2, own, lat), BF16),
            vmem((seqs, own, lat), BF16),
            vmem((nz, heads, 128), F32),
            vmem((nz, heads, 128), F32),
            vmem((seqs, nz, 2 * heads, lat // 2), BF16),
            vmem((seqs, nz, 2 * heads, lat // 2), BF16),
            vmem((seqs // 2 * heads, lat), F32),
            vmem((2, ndp, seqs // 2 * heads, dv), BF16),
            vmem((2, ndp * seqs // 2 * heads, dv), F32),
            vmem((ndp * seqs * pieces, 128), F32),
            vmem((nctx, seqs * pieces, 128), BF16),
            vmem((nctx, seqs * pieces, 128), BF16),
            vmem((seqs * pieces, 128), F32),
            dma((6,)),
            dma((seqs,)),
            dma((seqs + 1, nz)),
            dma((seqs + 1, nz)),
            dma((seqs + 1,)),
            dma((seqs + 1,)),
            dma((seqs, 2)),
            dma((seqs, 2)),
            dma((nz,)),
            dma((nz,)),
            dma((seqs, nz)),
            dma((seqs, nz)),
            dma((2, ndp)),
            dma((2, ndp)),
            dma((nctx,)),
            dma((nctx,)),
        ],
        compiler_params=pltpu.CompilerParams(
            collective_id=0, has_side_effects=True, vmem_limit_bytes=60 << 20
        ),
        name="mla_decode",
    )(
        lengths,
        q_nope.reshape(seqs * heads, dn),
        q_rope.reshape(seqs * heads, rope),
        w_uk.reshape(heads * dn, lat),
        w_uv.reshape(heads * lat, dv),
        w_out.T,
        jnp.swapaxes(latent_cache, 1, 2),
    )


def solution(mesh):
    in_specs = (
        P("dp", "ctx", None),
        P("dp", "ctx", None),
        P("ctx", None, None),
        P("ctx", None, None),
        P("ctx", "dp"),
        P("dp", "ctx", None),
        P("dp"),
    )
    out_specs = P("ctx", "dp")
    return jax.shard_map(
        functools.partial(per_device, mesh.shape["ctx"] // 2, mesh.shape["dp"]),
        mesh=mesh,
        in_specs=in_specs,
        out_specs=out_specs,
        check_vma=False,
    )
```
